128 devices in a mesh: grp: 4 (over z), fsdp: 32 (over y, x, core).
Axes of the slice: x: 4, y: 4, z: 4, core: 2. Of those that a mesh axis runs over, the one named last changes fastest.
Arguments:
- gradient: float32 [128, 262144], P(None, ('grp', 'fsdp')), may hold values from -1.5 to 1.5
- slot_block: int32 [256], replicated, may hold values from -1 to 127, as said below
- left_statistics: float32 [256, 512, 512], P(('grp', 'fsdp')), may hold values from -6 to 6
- right_statistics: float32 [256, 512, 512], P(('grp', 'fsdp')), may hold values from -6 to 6
- root_left: bfloat16 [256, 512, 512], P(('grp', 'fsdp')), may hold values from -2 to 2
- root_right: bfloat16 [256, 512, 512], P(('grp', 'fsdp')), may hold values from -2 to 2
Outputs:
- direction: bfloat16 [128, 262144], P(None, ('grp', 'fsdp'))
- new_left: float32 [256, 512, 512], P(('grp', 'fsdp'))
- new_right: float32 [256, 512, 512], P(('grp', 'fsdp'))
The draws below stay inside these ranges and needn't reach their ends.
Inputs may be any that keep to these rules, and one draw needn't show every extreme that they name: `slot_block`: every block index 0 to 127 stands in exactly one slot; -1 marks a free slot. Slots q * 2 to q * 2 + 1 are those of device q along grp+fsdp. Devices own 0 to 2 blocks, and some device owns 2.
All inputs are finite; a program needn't handle non-finite values.
Results may differ from the reference program's by a relative error of at most 0.006.
Values may be sent and summed in bfloat16 or wider, within the bound.
A program may use at most 64 MiB of HBM per device.

```python
import math
from functools import partial
import jax
import jax.numpy as jnp
from jax import lax

BLOCK_ORDER_SIZE = 512
OWNED_BLOCK_LIMIT = 2
TOTAL_BLOCKS = 128
FACTOR_SLOTS = 256


def draw_gradient(key, part):
    key = jax.random.fold_in(key, 5)
    first_draw, second_draw, third = jax.random.split(key, 3)
    base = jnp.clip(jax.random.normal(first_draw, (TOTAL_BLOCKS, BLOCK_ORDER_SIZE, BLOCK_ORDER_SIZE), jnp.float32), -3.0, 3.0)
    row_scale = jnp.exp(jax.random.uniform(second_draw, (TOTAL_BLOCKS, BLOCK_ORDER_SIZE, 1), jnp.float32, math.log(0.3), math.log(3.0)))
    col_scale = jnp.exp(jax.random.uniform(third, (TOTAL_BLOCKS, 1, BLOCK_ORDER_SIZE), jnp.float32, math.log(0.3), math.log(3.0)))
    return jnp.clip(base * row_scale * col_scale * 0.06, -1.5, 1.5).reshape(TOTAL_BLOCKS, BLOCK_ORDER_SIZE * BLOCK_ORDER_SIZE)


def make_root(key, load_spread):
    first_draw, second_draw = jax.random.split(key)
    random_noise = jnp.clip(jax.random.normal(first_draw, (FACTOR_SLOTS, BLOCK_ORDER_SIZE, BLOCK_ORDER_SIZE), jnp.float32), -4.0, 4.0) * (load_spread / math.sqrt(BLOCK_ORDER_SIZE))
    symmetric = 0.5 * (random_noise + jnp.swapaxes(random_noise, 1, 2))
    diagonal_entries = jax.random.uniform(second_draw, (FACTOR_SLOTS, BLOCK_ORDER_SIZE, 1), jnp.float32, 0.5, 1.5)
    return symmetric + diagonal_entries * jnp.eye(BLOCK_ORDER_SIZE, dtype=jnp.float32)


def draw_root_left(key, part):
    key = jax.random.fold_in(key, 7)
    return make_root(key, 0.5).astype(jnp.bfloat16)


def draw_root_right(key, part):
    key = jax.random.fold_in(key, 9)
    return make_root(key, 0.5).astype(jnp.bfloat16)


def draw_slot_block(key, part):
    key = jax.random.fold_in(key, 11)
    first_draw, second_draw, third, fourth_draw = jax.random.split(key, 4)
    device_list = FACTOR_SLOTS // OWNED_BLOCK_LIMIT
    paired = device_list // 2
    loads = jax.random.randint(first_draw, (paired,), 0, OWNED_BLOCK_LIMIT + 1).astype(jnp.int32)
    loads = loads.at[0].set(OWNED_BLOCK_LIMIT)
    loads_all = jnp.concatenate([loads, OWNED_BLOCK_LIMIT - loads])
    shuffle = jax.random.permutation(second_draw, device_list)
    device_load = jnp.zeros((device_list,), jnp.int32).at[shuffle].set(loads_all)
    scores = jax.random.randint(third, (device_list, OWNED_BLOCK_LIMIT), 0, 4096).astype(jnp.int32) * OWNED_BLOCK_LIMIT + jnp.arange(OWNED_BLOCK_LIMIT, dtype=jnp.int32)[None, :]
    ranks = jnp.argsort(jnp.argsort(scores, axis=1), axis=1)
    occupied = (ranks < device_load[:, None]).reshape(-1)
    spread_rating = jax.random.randint(fourth_draw, (FACTOR_SLOTS,), 0, 4096).astype(jnp.int32) * FACTOR_SLOTS + jnp.arange(FACTOR_SLOTS, dtype=jnp.int32)
    sort_key = jnp.where(occupied, 0, 1).astype(jnp.int32) * (1 << 30) + spread_rating
    picked_device = jnp.argsort(sort_key)[:TOTAL_BLOCKS]
    return jnp.full((FACTOR_SLOTS,), -1, jnp.int32).at[picked_device].set(jnp.arange(TOTAL_BLOCKS, dtype=jnp.int32))


def shard_levels(stream_key, shape, cuts, smallest, largest):
    def one(axis_at, parts):
        heights = jax.random.uniform(jax.random.fold_in(jax.random.fold_in(stream_key, 6), axis_at), (parts,), jnp.float32, smallest / len(cuts), largest / len(cuts))
        return jnp.repeat(jnp.exp(heights), shape[axis_at] // parts).reshape((-1,) + (1,) * (len(shape) - axis_at - 1))

    factor_of = one(*cuts[0])
    for cut in cuts[1:]:
        factor_of = factor_of * one(*cut)
    return factor_of


def noise(key, shape, width, limit, pieces=(), kind=jnp.bfloat16):
    array = width * jax.random.normal(key, shape, jnp.float32)
    if pieces:
        array = array * shard_levels(key, shape, pieces, -0.22, 0.18)
    return jnp.clip(array, -limit, limit).astype(kind)


def setup_inputs(seed: int = 0) -> dict:
    streams_of = jax.random.split(jax.random.key(seed), 7)
    return {
        "gradient": draw_gradient(jax.random.fold_in(streams_of[6], 71), 0),
        "slot_block": draw_slot_block(jax.random.fold_in(streams_of[6], 71), 0),
        "left_statistics": noise(streams_of[2], (FACTOR_SLOTS, BLOCK_ORDER_SIZE, BLOCK_ORDER_SIZE), 1.0, 6.0, ((0, 128),), jnp.float32),
        "right_statistics": noise(streams_of[3], (FACTOR_SLOTS, BLOCK_ORDER_SIZE, BLOCK_ORDER_SIZE), 1.0, 6.0, ((0, 128),), jnp.float32),
        "root_left": draw_root_left(jax.random.fold_in(streams_of[6], 71), 0),
        "root_right": draw_root_right(jax.random.fold_in(streams_of[6], 71), 0),
    }


decay_rate = 0.95
epsilon = 1e-06

def one_slot(gradient, packed):
    block_id, left_stat, right_stat, left_root, right_root = packed
    occupied = block_id >= 0
    picked = lax.dynamic_index_in_dim(gradient, jnp.maximum(block_id, 0).astype(jnp.int32), 0, keepdims=False)
    tile = jnp.where(occupied, picked, jnp.zeros_like(picked)).reshape(BLOCK_ORDER_SIZE, BLOCK_ORDER_SIZE)
    fresh_left = decay_rate * left_stat + jnp.dot(tile, tile.T, precision=lax.Precision.HIGHEST)
    fresh_right = decay_rate * right_stat + jnp.dot(tile.T, tile, precision=lax.Precision.HIGHEST)
    left_half = jnp.dot(left_root, tile.astype(jnp.bfloat16), preferred_element_type=jnp.float32).astype(jnp.bfloat16)
    shaped = jnp.dot(left_half, right_root, preferred_element_type=jnp.float32)
    grad_norm = jnp.sqrt(jnp.sum(tile * tile))
    shaped_norm = jnp.sqrt(jnp.sum(shaped * shaped))
    moved = (shaped * (grad_norm / (shaped_norm + epsilon))).astype(jnp.bfloat16)
    return (fresh_left, fresh_right, moved.reshape(BLOCK_ORDER_SIZE * BLOCK_ORDER_SIZE))

def reference(gradient, slot_block, left_statistics, right_statistics, root_left, root_right):
    new_left, new_right, moved = lax.map(partial(one_slot, gradient), (slot_block, left_statistics, right_statistics, root_left, root_right))
    target = jnp.where(slot_block >= 0, slot_block, TOTAL_BLOCKS).astype(jnp.int32)
    inverse = jnp.zeros((TOTAL_BLOCKS,), jnp.int32).at[target].set(jnp.arange(slot_block.shape[0], dtype=jnp.int32), mode='drop')
    direction = moved[inverse]
    return (direction, new_left, new_right)
```

```python
import jax
import jax.numpy as jnp
from jax import lax
from jax.experimental import pallas as pl
from jax.experimental.pallas import tpu as pltpu
from jax.sharding import PartitionSpec as P

decay_rate = 0.95
epsilon = 1e-06

BLOCKS = 128
SLOTS = 2
ORDER = 512
ROWS, LANES = 16, 128
GROUPS, Y, X, CORES = 4, 4, 4, 2
DEVICES = GROUPS * Y * X * CORES
LOGICAL = pl.DeviceIdType.LOGICAL


def far_first():
    ring = (0, 1, 2, 1)

    def hops(offset):
        return ring[offset // 32] + ring[offset // 8 % 4] + ring[offset // 2 % 4] + 0.1 * (offset % 2)

    return sorted(range(1, DEVICES), key=lambda offset: (-hops(offset), offset))


def kernel(
    slot_block, gradient, left_stat, right_stat, root_left, root_right,
    direction, new_left, new_right,
    rows_in, chunks_wide, chunks, outgoing, arrived, wide, tiles, half, moved, returned, wide_out,
    left_in, right_in, roots_l, roots_r, place_v, place_s,
    load_sem, stat_sem, place_sem, send_sem, recv_sem,
):
    g = lax.axis_index("grp")
    f = lax.axis_index("fsdp")
    me = g * 32 + f
    y, x, c = f // 8, lax.rem(f // 2, 4), lax.rem(f, 2)
    zs = [lax.rem(g + i, 4) * 32 for i in range(4)]
    ys = [lax.rem(y + i, 4) * 8 for i in range(4)]
    xs = [lax.rem(x + i, 4) * 2 for i in range(4)]
    cs = [lax.rem(c + i, 2) for i in range(2)]
    zy = [[a + b for b in ys] for a in zs]
    xc = [[a + b for b in cs] for a in xs]
    offsets = far_first()

    def device(offset):
        return zy[offset // 32][offset // 8 % 4] + xc[offset // 2 % 4][offset % 2]

    load = pltpu.make_async_copy(gradient, rows_in, load_sem.at[0])
    load.start()
    barrier = pltpu.get_barrier_semaphore()
    for offset in offsets:
        pl.semaphore_signal(barrier, inc=1, device_id=device(offset), device_id_type=LOGICAL)
    load_l = pltpu.make_async_copy(root_left, roots_l, load_sem.at[1])
    load_r = pltpu.make_async_copy(root_right, roots_r, load_sem.at[2])
    load_sl = pltpu.make_async_copy(left_stat, left_in, stat_sem.at[0])
    load_sr = pltpu.make_async_copy(right_stat, right_in, stat_sem.at[1])
    load_l.start()
    load_r.start()
    load_sl.start()
    load_sr.start()

    chunks[BLOCKS] = jnp.zeros((ROWS, LANES), jnp.bfloat16)
    load.wait()
    for j in range(ROWS):
        chunks_wide[pl.ds(j, BLOCKS, stride=ROWS), :] = rows_in[:, j * LANES : (j + 1) * LANES]

    def narrow(i, carry):
        chunks[pl.ds(i * 8, 8)] = (
            chunks_wide[pl.ds(pl.multiple_of(i * 128, 128), 128), :].astype(jnp.bfloat16).reshape(8, ROWS, LANES)
        )
        return carry

    lax.fori_loop(0, BLOCKS // 8, narrow, 0)

    def stage(s):
        def one(d, carry):
            block = slot_block[d * SLOTS + s]
            outgoing[s, d] = chunks[jnp.where(block < 0, BLOCKS, block)]
            return carry

        lax.fori_loop(0, DEVICES, one, 0, unroll=8)

    def send(i, source, target, s):
        for offset in offsets:
            d = device(offset)
            pltpu.make_async_remote_copy(
                src_ref=source.at[s, d],
                dst_ref=target.at[s, me],
                send_sem=send_sem.at[i],
                recv_sem=recv_sem.at[i],
                device_id=d,
                device_id_type=LOGICAL,
            ).start()
        target[s, me] = source[s, me]

    def wait(sems, i, buffer, s):
        part = buffer.at[s, pl.ds(0, DEVICES - 1)]
        pltpu.make_async_copy(part, part, sems.at[i]).wait()

    stage(0)
    pl.semaphore_wait(barrier, DEVICES - 1)
    send(0, outgoing, arrived, 0)
    stage(1)
    send(1, outgoing, arrived, 1)

    lanes = lax.broadcasted_iota(jnp.int32, (8, BLOCKS), 1)

    def find(q, found):
        return jnp.where(lanes == slot_block[q], q, found)

    place_v[...] = lax.fori_loop(0, DEVICES * SLOTS, find, jnp.zeros((8, BLOCKS), jnp.int32), unroll=8)
    place = pltpu.make_async_copy(place_v, place_s, place_sem)
    place.start()
    load_l.wait()
    load_r.wait()

    def precondition(s):
        def widen(i, carry):
            wide[pl.ds(pl.multiple_of(i * 128, 128), 128), :] = (
                arrived[s, pl.ds(i * 8, 8)].astype(jnp.float32).reshape(128, LANES)
            )
            return carry

        lax.fori_loop(0, DEVICES // 8, widen, 0)
        squares = jnp.zeros((8, LANES), jnp.float32)
        for j in range(ORDER // LANES):
            part = wide[pl.ds(j, ORDER, stride=4), :]
            squares += jnp.sum((part * part).reshape(ORDER // 8, 8, LANES), axis=0)
            tiles[s, :, j * LANES : (j + 1) * LANES] = part.astype(jnp.bfloat16)
        half[...] = jnp.dot(roots_l[s], tiles[s], preferred_element_type=jnp.float32).astype(jnp.bfloat16)
        shaped_squares = jnp.zeros((8, LANES), jnp.float32)
        for n in range(2):
            shaped = jnp.dot(
                half[...], roots_r[s, :, n * 256 : (n + 1) * 256], preferred_element_type=jnp.float32
            )
            for m in range(2):
                part = shaped[:, m * LANES : (m + 1) * LANES]
                shaped_squares += jnp.sum((part * part).reshape(ORDER // 8, 8, LANES), axis=0)
                wide[pl.ds(n * 2 + m, ORDER, stride=4), :] = part
        grad_norm = jnp.sqrt(jnp.sum(squares, keepdims=True))
        shaped_norm = jnp.sqrt(jnp.sum(shaped_squares, keepdims=True))
        scale = grad_norm / (shaped_norm + epsilon)

        def pack(i, carry):
            moved[s, pl.ds(i * 8, 8)] = (
                (wide[pl.ds(pl.multiple_of(i * 128, 128), 128), :] * scale)
                .astype(jnp.bfloat16)
                .reshape(8, ROWS, LANES)
            )
            return carry

        lax.fori_loop(0, DEVICES // 8, pack, 0)

    for s in range(SLOTS):
        wait(recv_sem, s, arrived, s)
        precondition(s)
        send(2 + s, moved, returned, s)

    load_sl.wait()
    load_sr.wait()
    for s in range(SLOTS):
        tile = tiles[s]
        new_left[s] = decay_rate * left_in[s] + lax.dot_general(
            tile, tile, (((1,), (1,)), ((), ())), preferred_element_type=jnp.float32
        )
        new_right[s] = decay_rate * right_in[s] + lax.dot_general(
            tile, tile, (((0,), (0,)), ((), ())), preferred_element_type=jnp.float32
        )
    place.wait()
    wait(recv_sem, 2, returned, 0)
    wait(recv_sem, 3, returned, 1)

    def gather(k, carry):
        q = place_s[0, k]
        wide_out[pl.ds(pl.multiple_of(k * ROWS, ROWS), ROWS), :] = returned[lax.rem(q, 2), q // 2].astype(jnp.float32)
        return carry

    lax.fori_loop(0, BLOCKS, gather, 0, unroll=8)
    for j in range(ROWS):
        direction[:, j * LANES : (j + 1) * LANES] = wide_out[pl.ds(j, BLOCKS, stride=ROWS), :].astype(jnp.bfloat16)
    for s in range(SLOTS):
        wait(send_sem, s, outgoing, s)
        wait(send_sem, 2 + s, moved, s)


def body(gradient, slot_block, left_statistics, right_statistics, root_left, root_right):
    anywhere = pl.BlockSpec(memory_space=pltpu.HBM)
    chunk = (ROWS, LANES)
    square = (SLOTS, ORDER, ORDER)
    flops = 2 * 4 * SLOTS * ORDER**3
    direction, new_left, new_right = pl.pallas_call(
        kernel,
        out_shape=(
            pltpu.VMEM((BLOCKS, ROWS * LANES), jnp.bfloat16),
            pltpu.VMEM(square, jnp.float32),
            pltpu.VMEM(square, jnp.float32),
        ),
        in_specs=[pl.BlockSpec(memory_space=pltpu.SMEM)] + [anywhere] * 5,
        out_specs=tuple(pl.BlockSpec(memory_space=pltpu.VMEM) for _ in range(3)),
        scratch_shapes=[
            pltpu.VMEM((BLOCKS, ROWS * LANES), jnp.float32),
            pltpu.VMEM((BLOCKS * ROWS, LANES), jnp.float32),
            pltpu.VMEM((BLOCKS + 1,) + chunk, jnp.bfloat16),
            pltpu.VMEM((SLOTS, DEVICES) + chunk, jnp.bfloat16),
            pltpu.VMEM((SLOTS, DEVICES) + chunk, jnp.bfloat16),
            pltpu.VMEM((DEVICES * ROWS, LANES), jnp.float32),
            pltpu.VMEM(square, jnp.bfloat16),
            pltpu.VMEM((ORDER, ORDER), jnp.bfloat16),
            pltpu.VMEM((SLOTS, DEVICES) + chunk, jnp.bfloat16),
            pltpu.VMEM((SLOTS, DEVICES) + chunk, jnp.bfloat16),
            pltpu.VMEM((BLOCKS * ROWS, LANES), jnp.float32),
            pltpu.VMEM(square, jnp.float32),
            pltpu.VMEM(square, jnp.float32),
            pltpu.VMEM(square, jnp.bfloat16),
            pltpu.VMEM(square, jnp.bfloat16),
            pltpu.VMEM((8, BLOCKS), jnp.int32),
            pltpu.SMEM((8, BLOCKS), jnp.int32),
            pltpu.SemaphoreType.DMA((3,)),
            pltpu.SemaphoreType.DMA((2,)),
            pltpu.SemaphoreType.DMA,
            pltpu.SemaphoreType.DMA((4,)),
            pltpu.SemaphoreType.DMA((4,)),
        ],
        compiler_params=pltpu.CompilerParams(
            collective_id=0, has_side_effects=True, vmem_limit_bytes=56 * 2**20
        ),
        cost_estimate=pl.CostEstimate(flops=flops, bytes_accessed=12 * 2**20, transcendentals=0),
    )(slot_block, gradient, left_statistics, right_statistics, root_left, root_right)
    return (direction, new_left, new_right)


def solution(mesh):
    placed = (
        P(None, ("grp", "fsdp")),
        P(),
        P(("grp", "fsdp"), None, None),
        P(("grp", "fsdp"), None, None),
        P(("grp", "fsdp"), None, None),
        P(("grp", "fsdp"), None, None),
    )
    return jax.shard_map(
        body,
        mesh=mesh,
        in_specs=placed,
        out_specs=(
            P(None, ("grp", "fsdp")),
            P(("grp", "fsdp"), None, None),
            P(("grp", "fsdp"), None, None),
        ),
        check_vma=False,
    )
```

```python
import jax
import jax.numpy as jnp
from jax import lax
from jax.experimental import pallas as pl
from jax.experimental.pallas import tpu as pltpu
from jax.sharding import PartitionSpec as P

decay_rate = 0.95
epsilon = 1e-06

BLOCKS = 128
SLOTS = 2
ORDER = 512
ROWS, LANES = 16, 128
GROUPS, Y, X, CORES = 4, 4, 4, 2
DEVICES = GROUPS * Y * X * CORES
LOGICAL = pl.DeviceIdType.LOGICAL


def far_first():
    ring = (0, 1, 2, 1)

    def hops(offset):
        return ring[offset // 32] + ring[offset // 8 % 4] + ring[offset // 2 % 4] + 0.1 * (offset % 2)

    return sorted(range(1, DEVICES), key=lambda offset: (-hops(offset), offset))


def kernel(
    slot_block, gradient, left_stat, right_stat, root_left, root_right,
    returned, new_left, new_right,
    rows_in, chunks_wide, chunks, outgoing, arrived, wide, tiles, half, moved,
    left_in, right_in, roots_l, roots_r,
    load_sem, stat_sem, send_sem, recv_sem,
):
    g = lax.axis_index("grp")
    f = lax.axis_index("fsdp")
    me = g * 32 + f
    y, x, c = f // 8, lax.rem(f // 2, 4), lax.rem(f, 2)
    zs = [lax.rem(g + i, 4) * 32 for i in range(4)]
    ys = [lax.rem(y + i, 4) * 8 for i in range(4)]
    xs = [lax.rem(x + i, 4) * 2 for i in range(4)]
    cs = [lax.rem(c + i, 2) for i in range(2)]
    zy = [[a + b for b in ys] for a in zs]
    xc = [[a + b for b in cs] for a in xs]
    offsets = far_first()

    def device(offset):
        return zy[offset // 32][offset // 8 % 4] + xc[offset // 2 % 4][offset % 2]

    load = pltpu.make_async_copy(gradient, rows_in, load_sem.at[0])
    load.start()
    barrier = pltpu.get_barrier_semaphore()
    for offset in offsets:
        pl.semaphore_signal(barrier, inc=1, device_id=device(offset), device_id_type=LOGICAL)
    load_l = pltpu.make_async_copy(root_left, roots_l, load_sem.at[1])
    load_r = pltpu.make_async_copy(root_right, roots_r, load_sem.at[2])
    load_sl = pltpu.make_async_copy(left_stat, left_in, stat_sem.at[0])
    load_sr = pltpu.make_async_copy(right_stat, right_in, stat_sem.at[1])
    load_l.start()
    load_r.start()
    load_sl.start()
    load_sr.start()

    chunks[BLOCKS] = jnp.zeros((ROWS, LANES), jnp.bfloat16)
    load.wait()
    for j in range(ROWS):
        chunks_wide[pl.ds(j, BLOCKS, stride=ROWS), :] = rows_in[:, j * LANES : (j + 1) * LANES]

    def narrow(i, carry):
        chunks[pl.ds(i * 8, 8)] = (
            chunks_wide[pl.ds(pl.multiple_of(i * 128, 128), 128), :].astype(jnp.bfloat16).reshape(8, ROWS, LANES)
        )
        return carry

    lax.fori_loop(0, BLOCKS // 8, narrow, 0)

    def stage(s):
        def one(d, carry):
            block = slot_block[d * SLOTS + s]
            outgoing[s, d] = chunks[jnp.where(block < 0, BLOCKS, block)]
            return carry

        lax.fori_loop(0, DEVICES, one, 0, unroll=8)

    def send(i, source, target, s):
        for offset in offsets:
            d = device(offset)
            pltpu.make_async_remote_copy(
                src_ref=source.at[s, d],
                dst_ref=target.at[s, me],
                send_sem=send_sem.at[i],
                recv_sem=recv_sem.at[i],
                device_id=d,
                device_id_type=LOGICAL,
            ).start()
        target[s, me] = source[s, me]

    def wait(sems, i, buffer, s):
        part = buffer.at[s, pl.ds(0, DEVICES - 1)]
        pltpu.make_async_copy(part, part, sems.at[i]).wait()

    stage(0)
    stage(1)
    pl.semaphore_wait(barrier, DEVICES - 1)
    send(0, outgoing, arrived, 0)
    send(1, outgoing, arrived, 1)

    load_l.wait()
    load_r.wait()

    def precondition(s):
        def widen(i, carry):
            wide[pl.ds(pl.multiple_of(i * 128, 128), 128), :] = (
                arrived[s, pl.ds(i * 8, 8)].astype(jnp.float32).reshape(128, LANES)
            )
            return carry

        lax.fori_loop(0, DEVICES // 8, widen, 0)
        squares = jnp.zeros((8, LANES), jnp.float32)
        for j in range(ORDER // LANES):
            part = wide[pl.ds(j, ORDER, stride=4), :]
            squares += jnp.sum((part * part).reshape(ORDER // 8, 8, LANES), axis=0)
            tiles[s, :, j * LANES : (j + 1) * LANES] = part.astype(jnp.bfloat16)
        half[...] = jnp.dot(roots_l[s], tiles[s], preferred_element_type=jnp.float32).astype(jnp.bfloat16)
        shaped_squares = jnp.zeros((8, LANES), jnp.float32)
        for n in range(2):
            shaped = jnp.dot(
                half[...], roots_r[s, :, n * 256 : (n + 1) * 256], preferred_element_type=jnp.float32
            )
            for m in range(2):
                part = shaped[:, m * LANES : (m + 1) * LANES]
                shaped_squares += jnp.sum((part * part).reshape(ORDER // 8, 8, LANES), axis=0)
                wide[pl.ds(n * 2 + m, ORDER, stride=4), :] = part
        grad_norm = jnp.sqrt(jnp.sum(squares, keepdims=True))
        shaped_norm = jnp.sqrt(jnp.sum(shaped_squares, keepdims=True))
        scale = grad_norm / (shaped_norm + epsilon)

        def pack(i, carry):
            moved[s, pl.ds(i * 8, 8)] = (
                (wide[pl.ds(pl.multiple_of(i * 128, 128), 128), :] * scale)
                .astype(jnp.bfloat16)
                .reshape(8, ROWS, LANES)
            )
            return carry

        lax.fori_loop(0, DEVICES // 8, pack, 0)

    for s in range(SLOTS):
        wait(recv_sem, s, arrived, s)
        precondition(s)
        send(2 + s, moved, returned, s)

    load_sl.wait()
    load_sr.wait()
    for s in range(SLOTS):
        tile = tiles[s]
        new_left[s] = decay_rate * left_in[s] + lax.dot_general(
            tile, tile, (((1,), (1,)), ((), ())), preferred_element_type=jnp.float32
        )
        new_right[s] = decay_rate * right_in[s] + lax.dot_general(
            tile, tile, (((0,), (0,)), ((), ())), preferred_element_type=jnp.float32
        )
    wait(recv_sem, 2, returned, 0)
    wait(recv_sem, 3, returned, 1)
    for s in range(SLOTS):
        wait(send_sem, s, outgoing, s)
        wait(send_sem, 2 + s, moved, s)


def finish(slot_block, returned, left, right, direction, new_left, new_right, wide_out, rows_out, out_sem):
    copies = [
        pltpu.make_async_copy(source.at[s], target.at[s], out_sem.at[2 * i + s])
        for i, (source, target) in enumerate(((left, new_left), (right, new_right)))
        for s in range(SLOTS)
    ]
    for copy in copies:
        copy.start()

    def place(d, carry):
        for s in range(SLOTS):
            block = slot_block[d * SLOTS + s]
            wide_out[jnp.where(block < 0, BLOCKS, block)] = returned[s, d].astype(jnp.float32)
        return carry

    lax.fori_loop(0, DEVICES, place, 0, unroll=8)
    rows = wide_out.reshape((BLOCKS + 1) * ROWS, LANES)
    for j in range(ROWS):
        rows_out[:, j * LANES : (j + 1) * LANES] = rows[pl.ds(j, BLOCKS, stride=ROWS), :].astype(jnp.bfloat16)
    last = pltpu.make_async_copy(rows_out, direction, out_sem.at[4])
    last.start()
    for copy in copies:
        copy.wait()
    last.wait()


def body(gradient, slot_block, left_statistics, right_statistics, root_left, root_right):
    anywhere = pl.BlockSpec(memory_space=pltpu.HBM)
    chunk = (ROWS, LANES)
    square = (SLOTS, ORDER, ORDER)
    flops = 2 * 4 * SLOTS * ORDER**3
    returned, left, right = pl.pallas_call(
        kernel,
        out_shape=(
            pltpu.VMEM((SLOTS, DEVICES) + chunk, jnp.bfloat16),
            pltpu.VMEM(square, jnp.float32),
            pltpu.VMEM(square, jnp.float32),
        ),
        in_specs=[pl.BlockSpec(memory_space=pltpu.SMEM)] + [anywhere] * 5,
        out_specs=tuple(pl.BlockSpec(memory_space=pltpu.VMEM) for _ in range(3)),
        scratch_shapes=[
            pltpu.VMEM((BLOCKS, ROWS * LANES), jnp.float32),
            pltpu.VMEM((BLOCKS * ROWS, LANES), jnp.float32),
            pltpu.VMEM((BLOCKS + 1,) + chunk, jnp.bfloat16),
            pltpu.VMEM((SLOTS, DEVICES) + chunk, jnp.bfloat16),
            pltpu.VMEM((SLOTS, DEVICES) + chunk, jnp.bfloat16),
            pltpu.VMEM((DEVICES * ROWS, LANES), jnp.float32),
            pltpu.VMEM(square, jnp.bfloat16),
            pltpu.VMEM((ORDER, ORDER), jnp.bfloat16),
            pltpu.VMEM((SLOTS, DEVICES) + chunk, jnp.bfloat16),
            pltpu.VMEM(square, jnp.float32),
            pltpu.VMEM(square, jnp.float32),
            pltpu.VMEM(square, jnp.bfloat16),
            pltpu.VMEM(square, jnp.bfloat16),
            pltpu.SemaphoreType.DMA((3,)),
            pltpu.SemaphoreType.DMA((2,)),
            pltpu.SemaphoreType.DMA((4,)),
            pltpu.SemaphoreType.DMA((4,)),
        ],
        compiler_params=pltpu.CompilerParams(
            collective_id=0, has_side_effects=True, vmem_limit_bytes=56 * 2**20
        ),
        cost_estimate=pl.CostEstimate(flops=flops, bytes_accessed=12 * 2**20, transcendentals=0),
    )(slot_block, gradient, left_statistics, right_statistics, root_left, root_right)
    in_vmem = pl.BlockSpec(memory_space=pltpu.VMEM)
    return pl.pallas_call(
        finish,
        out_shape=(
            jax.ShapeDtypeStruct((BLOCKS, ROWS * LANES), jnp.bfloat16),
            jax.ShapeDtypeStruct(square, jnp.float32),
            jax.ShapeDtypeStruct(square, jnp.float32),
        ),
        in_specs=[pl.BlockSpec(memory_space=pltpu.SMEM)] + [in_vmem] * 3,
        out_specs=(anywhere,) * 3,
        scratch_shapes=[
            pltpu.VMEM((BLOCKS + 1,) + chunk, jnp.float32),
            pltpu.VMEM((BLOCKS, ROWS * LANES), jnp.bfloat16),
            pltpu.SemaphoreType.DMA((5,)),
        ],
        compiler_params=pltpu.CompilerParams(vmem_limit_bytes=16 * 2**20),
    )(slot_block, returned, left, right)


def solution(mesh):
    placed = (
        P(None, ("grp", "fsdp")),
        P(),
        P(("grp", "fsdp"), None, None),
        P(("grp", "fsdp"), None, None),
        P(("grp", "fsdp"), None, None),
        P(("grp", "fsdp"), None, None),
    )
    return jax.shard_map(
        body,
        mesh=mesh,
        in_specs=placed,
        out_specs=(
            P(None, ("grp", "fsdp")),
            P(("grp", "fsdp"), None, None),
            P(("grp", "fsdp"), None, None),
        ),
        check_vma=False,
    )
```

```python
import jax
import jax.numpy as jnp
from jax import lax
from jax.experimental import pallas as pl
from jax.experimental.pallas import tpu as pltpu
from jax.sharding import PartitionSpec as P

decay_rate = 0.95
epsilon = 1e-06

BLOCKS = 128
SLOTS = 2
ORDER = 512
ROWS, LANES = 16, 128
GROUPS, Y, X, CORES = 4, 4, 4, 2
DEVICES = GROUPS * Y * X * CORES
LOGICAL = pl.DeviceIdType.LOGICAL


def far_first():
    ring = (0, 1, 2, 1)

    def hops(offset):
        return ring[offset // 32] + ring[offset // 8 % 4] + ring[offset // 2 % 4] + 0.1 * (offset % 2)

    return sorted(range(1, DEVICES), key=lambda offset: (-hops(offset), offset))


def apart(offset):
    return sum(step > 0 for step in (offset // 32, offset // 8 % 4, offset // 2 % 4))


def kernel(
    slot_block, gradient, left_stat, right_stat, root_left, root_right,
    returned, new_left, new_right,
    rows_in, chunks_wide, chunks, outgoing, arrived, wide, tiles, half, moved,
    left_in, right_in, roots_l, roots_r,
    load_sem, stat_sem, send_sem, recv_sem, round_sem,
):
    g = lax.axis_index("grp")
    f = lax.axis_index("fsdp")
    me = g * 32 + f
    y, x, c = f // 8, lax.rem(f // 2, 4), lax.rem(f, 2)
    zs = [lax.rem(g + i, 4) * 32 for i in range(4)]
    ys = [lax.rem(y + i, 4) * 8 for i in range(4)]
    xs = [lax.rem(x + i, 4) * 2 for i in range(4)]
    cs = [lax.rem(c + i, 2) for i in range(2)]
    zy = [[a + b for b in ys] for a in zs]
    xc = [[a + b for b in cs] for a in xs]
    offsets = far_first()

    def device(offset):
        return zy[offset // 32][offset // 8 % 4] + xc[offset // 2 % 4][offset % 2]

    load = pltpu.make_async_copy(gradient, rows_in, load_sem.at[0])
    load.start()
    barrier = pltpu.get_barrier_semaphore()
    near = [offset for offset in offsets if apart(offset) <= 2]
    lines = [offset for offset in near if offset % 2 == 0 and apart(offset) == 1]
    for offset in near:
        pl.semaphore_signal(barrier, inc=1, device_id=device(offset), device_id_type=LOGICAL)
    load_l = pltpu.make_async_copy(root_left, roots_l, load_sem.at[1])
    load_r = pltpu.make_async_copy(root_right, roots_r, load_sem.at[2])
    load_sl = pltpu.make_async_copy(left_stat, left_in, stat_sem.at[0])
    load_sr = pltpu.make_async_copy(right_stat, right_in, stat_sem.at[1])
    load_l.start()
    load_r.start()
    load_sl.start()
    load_sr.start()

    chunks[BLOCKS] = jnp.zeros((ROWS, LANES), jnp.bfloat16)
    load.wait()
    for j in range(ROWS):
        chunks_wide[pl.ds(j, BLOCKS, stride=ROWS), :] = rows_in[:, j * LANES : (j + 1) * LANES]

    def narrow(i, carry):
        chunks[pl.ds(i * 8, 8)] = (
            chunks_wide[pl.ds(pl.multiple_of(i * 128, 128), 128), :].astype(jnp.bfloat16).reshape(8, ROWS, LANES)
        )
        return carry

    lax.fori_loop(0, BLOCKS // 8, narrow, 0)

    def stage(s):
        def one(d, carry):
            block = slot_block[d * SLOTS + s]
            outgoing[s, d] = chunks[jnp.where(block < 0, BLOCKS, block)]
            return carry

        lax.fori_loop(0, DEVICES, one, 0, unroll=8)

    def send(i, source, target, s, offsets=offsets):
        for offset in offsets:
            d = device(offset)
            pltpu.make_async_remote_copy(
                src_ref=source.at[s, d],
                dst_ref=target.at[s, me],
                send_sem=send_sem.at[i],
                recv_sem=recv_sem.at[i],
                device_id=d,
                device_id_type=LOGICAL,
            ).start()

    def wait(sems, i, buffer, s):
        part = buffer.at[s, pl.ds(0, DEVICES - 1)]
        pltpu.make_async_copy(part, part, sems.at[i]).wait()

    stage(0)
    stage(1)
    for s in range(SLOTS):
        arrived[s, me] = outgoing[s, me]
    pl.semaphore_wait(barrier, len(near))
    for offset in lines:
        pl.semaphore_signal(round_sem, inc=1, device_id=device(offset), device_id_type=LOGICAL)
    send(0, outgoing, arrived, 0, [offset for offset in offsets if apart(offset) == 2])
    pl.semaphore_wait(round_sem, len(lines))
    send(0, outgoing, arrived, 0, [offset for offset in offsets if apart(offset) == 3])
    send(0, outgoing, arrived, 0, [offset for offset in offsets if apart(offset) <= 1])
    send(1, outgoing, arrived, 1)

    load_l.wait()
    load_r.wait()

    def precondition(s):
        def widen(i, carry):
            wide[pl.ds(pl.multiple_of(i * 128, 128), 128), :] = (
                arrived[s, pl.ds(i * 8, 8)].astype(jnp.float32).reshape(128, LANES)
            )
            return carry

        lax.fori_loop(0, DEVICES // 8, widen, 0)
        squares = jnp.zeros((8, LANES), jnp.float32)
        for j in range(ORDER // LANES):
            part = wide[pl.ds(j, ORDER, stride=4), :]
            squares += jnp.sum((part * part).reshape(ORDER // 8, 8, LANES), axis=0)
            tiles[s, :, j * LANES : (j + 1) * LANES] = part.astype(jnp.bfloat16)
        half[...] = jnp.dot(roots_l[s], tiles[s], preferred_element_type=jnp.float32).astype(jnp.bfloat16)
        shaped_squares = jnp.zeros((8, LANES), jnp.float32)
        for n in range(2):
            shaped = jnp.dot(
                half[...], roots_r[s, :, n * 256 : (n + 1) * 256], preferred_element_type=jnp.float32
            )
            for m in range(2):
                part = shaped[:, m * LANES : (m + 1) * LANES]
                shaped_squares += jnp.sum((part * part).reshape(ORDER // 8, 8, LANES), axis=0)
                wide[pl.ds(n * 2 + m, ORDER, stride=4), :] = part
        grad_norm = jnp.sqrt(jnp.sum(squares, keepdims=True))
        shaped_norm = jnp.sqrt(jnp.sum(shaped_squares, keepdims=True))
        scale = grad_norm / (shaped_norm + epsilon)

        def pack(i, carry):
            moved[s, pl.ds(i * 8, 8)] = (
                (wide[pl.ds(pl.multiple_of(i * 128, 128), 128), :] * scale)
                .astype(jnp.bfloat16)
                .reshape(8, ROWS, LANES)
            )
            return carry

        lax.fori_loop(0, DEVICES // 8, pack, 0)

    for s in range(SLOTS):
        wait(recv_sem, s, arrived, s)
        precondition(s)
        send(2 + s, moved, returned, s)
        returned[s, me] = moved[s, me]

    load_sl.wait()
    load_sr.wait()
    for s in range(SLOTS):
        tile = tiles[s]
        new_left[s] = decay_rate * left_in[s] + lax.dot_general(
            tile, tile, (((1,), (1,)), ((), ())), preferred_element_type=jnp.float32
        )
        new_right[s] = decay_rate * right_in[s] + lax.dot_general(
            tile, tile, (((0,), (0,)), ((), ())), preferred_element_type=jnp.float32
        )
    wait(recv_sem, 2, returned, 0)
    wait(recv_sem, 3, returned, 1)
    for s in range(SLOTS):
        wait(send_sem, s, outgoing, s)
        wait(send_sem, 2 + s, moved, s)


def finish(slot_block, returned, left, right, direction, new_left, new_right, wide_out, rows_out, out_sem):
    copies = [
        pltpu.make_async_copy(source.at[s], target.at[s], out_sem.at[2 * i + s])
        for i, (source, target) in enumerate(((left, new_left), (right, new_right)))
        for s in range(SLOTS)
    ]
    for copy in copies:
        copy.start()

    def place(d, carry):
        for s in range(SLOTS):
            block = slot_block[d * SLOTS + s]
            wide_out[jnp.where(block < 0, BLOCKS, block)] = returned[s, d].astype(jnp.float32)
        return carry

    lax.fori_loop(0, DEVICES, place, 0, unroll=8)
    rows = wide_out.reshape((BLOCKS + 1) * ROWS, LANES)
    for j in range(ROWS):
        rows_out[:, j * LANES : (j + 1) * LANES] = rows[pl.ds(j, BLOCKS, stride=ROWS), :].astype(jnp.bfloat16)
    last = pltpu.make_async_copy(rows_out, direction, out_sem.at[4])
    last.start()
    for copy in copies:
        copy.wait()
    last.wait()


def body(gradient, slot_block, left_statistics, right_statistics, root_left, root_right):
    anywhere = pl.BlockSpec(memory_space=pltpu.HBM)
    chunk = (ROWS, LANES)
    square = (SLOTS, ORDER, ORDER)
    flops = 2 * 4 * SLOTS * ORDER**3
    returned, left, right = pl.pallas_call(
        kernel,
        out_shape=(
            pltpu.VMEM((SLOTS, DEVICES) + chunk, jnp.bfloat16),
            pltpu.VMEM(square, jnp.float32),
            pltpu.VMEM(square, jnp.float32),
        ),
        in_specs=[pl.BlockSpec(memory_space=pltpu.SMEM)] + [anywhere] * 5,
        out_specs=tuple(pl.BlockSpec(memory_space=pltpu.VMEM) for _ in range(3)),
        scratch_shapes=[
            pltpu.VMEM((BLOCKS, ROWS * LANES), jnp.float32),
            pltpu.VMEM((BLOCKS * ROWS, LANES), jnp.float32),
            pltpu.VMEM((BLOCKS + 1,) + chunk, jnp.bfloat16),
            pltpu.VMEM((SLOTS, DEVICES) + chunk, jnp.bfloat16),
            pltpu.VMEM((SLOTS, DEVICES) + chunk, jnp.bfloat16),
            pltpu.VMEM((DEVICES * ROWS, LANES), jnp.float32),
            pltpu.VMEM(square, jnp.bfloat16),
            pltpu.VMEM((ORDER, ORDER), jnp.bfloat16),
            pltpu.VMEM((SLOTS, DEVICES) + chunk, jnp.bfloat16),
            pltpu.VMEM(square, jnp.float32),
            pltpu.VMEM(square, jnp.float32),
            pltpu.VMEM(square, jnp.bfloat16),
            pltpu.VMEM(square, jnp.bfloat16),
            pltpu.SemaphoreType.DMA((3,)),
            pltpu.SemaphoreType.DMA((2,)),
            pltpu.SemaphoreType.DMA((4,)),
            pltpu.SemaphoreType.DMA((4,)),
            pltpu.SemaphoreType.REGULAR,
        ],
        compiler_params=pltpu.CompilerParams(
            collective_id=0, has_side_effects=True, vmem_limit_bytes=56 * 2**20
        ),
        cost_estimate=pl.CostEstimate(flops=flops, bytes_accessed=12 * 2**20, transcendentals=0),
    )(slot_block, gradient, left_statistics, right_statistics, root_left, root_right)
    in_vmem = pl.BlockSpec(memory_space=pltpu.VMEM)
    return pl.pallas_call(
        finish,
        out_shape=(
            jax.ShapeDtypeStruct((BLOCKS, ROWS * LANES), jnp.bfloat16),
            jax.ShapeDtypeStruct(square, jnp.float32),
            jax.ShapeDtypeStruct(square, jnp.float32),
        ),
        in_specs=[pl.BlockSpec(memory_space=pltpu.SMEM)] + [in_vmem] * 3,
        out_specs=(anywhere,) * 3,
        scratch_shapes=[
            pltpu.VMEM((BLOCKS + 1,) + chunk, jnp.float32),
            pltpu.VMEM((BLOCKS, ROWS * LANES), jnp.bfloat16),
            pltpu.SemaphoreType.DMA((5,)),
        ],
        compiler_params=pltpu.CompilerParams(vmem_limit_bytes=16 * 2**20),
    )(slot_block, returned, left, right)


def solution(mesh):
    placed = (
        P(None, ("grp", "fsdp")),
        P(),
        P(("grp", "fsdp"), None, None),
        P(("grp", "fsdp"), None, None),
        P(("grp", "fsdp"), None, None),
        P(("grp", "fsdp"), None, None),
    )
    return jax.shard_map(
        body,
        mesh=mesh,
        in_specs=placed,
        out_specs=(
            P(None, ("grp", "fsdp")),
            P(("grp", "fsdp"), None, None),
            P(("grp", "fsdp"), None, None),
        ),
        check_vma=False,
    )
```

```python
import jax
import jax.numpy as jnp
from jax import lax
from jax.experimental import pallas as pl
from jax.experimental.pallas import tpu as pltpu
from jax.sharding import PartitionSpec as P

decay_rate = 0.95
epsilon = 1e-06

BLOCKS = 128
SLOTS = 2
ORDER = 512
ROWS, LANES = 16, 128
GROUPS, Y, X, CORES = 4, 4, 4, 2
DEVICES = GROUPS * Y * X * CORES
LOGICAL = pl.DeviceIdType.LOGICAL


def far_first():
    ring = (0, 1, 2, 1)

    def hops(offset):
        return ring[offset // 32] + ring[offset // 8 % 4] + ring[offset // 2 % 4] + 0.1 * (offset % 2)

    return sorted(range(1, DEVICES), key=lambda offset: (-hops(offset), offset))


def apart(offset):
    return sum(step > 0 for step in (offset // 32, offset // 8 % 4, offset // 2 % 4))


def kernel(
    blocks_in, gradient, left_stat, right_stat, root_left, root_right,
    returned, new_left, new_right,
    rows_in, chunks_wide, chunks, outgoing, arrived, wide, tiles, half, moved,
    left_in, right_in, roots_l, roots_r, slot_block,
    load_sem, stat_sem, send_sem, recv_sem, round_sem,
):
    g = lax.axis_index("grp")
    f = lax.axis_index("fsdp")
    me = g * 32 + f
    y, x, c = f // 8, lax.rem(f // 2, 4), lax.rem(f, 2)
    zs = [lax.rem(g + i, 4) * 32 for i in range(4)]
    ys = [lax.rem(y + i, 4) * 8 for i in range(4)]
    xs = [lax.rem(x + i, 4) * 2 for i in range(4)]
    cs = [lax.rem(c + i, 2) for i in range(2)]
    zy = [[a + b for b in ys] for a in zs]
    xc = [[a + b for b in cs] for a in xs]
    offsets = far_first()

    def device(offset):
        return zy[offset // 32][offset // 8 % 4] + xc[offset // 2 % 4][offset % 2]

    load = pltpu.make_async_copy(gradient, rows_in, load_sem.at[0])
    load.start()
    fetch = pltpu.make_async_copy(blocks_in, slot_block, load_sem.at[3])
    fetch.start()
    barrier = pltpu.get_barrier_semaphore()
    near = [offset for offset in offsets if apart(offset) <= 2]
    lines = [offset for offset in near if offset % 2 == 0 and apart(offset) == 1]
    for offset in near:
        pl.semaphore_signal(barrier, inc=1, device_id=device(offset), device_id_type=LOGICAL)
    load_l = pltpu.make_async_copy(root_left, roots_l, load_sem.at[1])
    load_r = pltpu.make_async_copy(root_right, roots_r, load_sem.at[2])
    load_sl = pltpu.make_async_copy(left_stat, left_in, stat_sem.at[0])
    load_sr = pltpu.make_async_copy(right_stat, right_in, stat_sem.at[1])
    load_l.start()
    load_r.start()
    load_sl.start()
    load_sr.start()

    chunks[BLOCKS] = jnp.zeros((ROWS, LANES), jnp.bfloat16)
    load.wait()
    for j in range(ROWS):
        chunks_wide[pl.ds(j, BLOCKS, stride=ROWS), :] = rows_in[:, j * LANES : (j + 1) * LANES]

    def narrow(i, carry):
        chunks[pl.ds(i * 8, 8)] = (
            chunks_wide[pl.ds(pl.multiple_of(i * 128, 128), 128), :].astype(jnp.bfloat16).reshape(8, ROWS, LANES)
        )
        return carry

    lax.fori_loop(0, BLOCKS // 8, narrow, 0)

    def stage(s):
        def one(d, carry):
            block = slot_block[d * SLOTS + s]
            outgoing[s, d] = chunks[jnp.where(block < 0, BLOCKS, block)]
            return carry

        lax.fori_loop(0, DEVICES, one, 0, unroll=8)

    def send(i, source, target, s, offsets=offsets):
        for offset in offsets:
            d = device(offset)
            pltpu.make_async_remote_copy(
                src_ref=source.at[s, d],
                dst_ref=target.at[s, me],
                send_sem=send_sem.at[i],
                recv_sem=recv_sem.at[i],
                device_id=d,
                device_id_type=LOGICAL,
            ).start()

    def wait(sems, i, buffer, s):
        part = buffer.at[s, pl.ds(0, DEVICES - 1)]
        pltpu.make_async_copy(part, part, sems.at[i]).wait()

    fetch.wait()
    stage(0)
    stage(1)
    for s in range(SLOTS):
        arrived[s, me] = outgoing[s, me]
    pl.semaphore_wait(barrier, len(near))
    for offset in lines:
        pl.semaphore_signal(round_sem, inc=1, device_id=device(offset), device_id_type=LOGICAL)
    send(0, outgoing, arrived, 0, [offset for offset in offsets if apart(offset) == 2])
    pl.semaphore_wait(round_sem, len(lines))
    send(0, outgoing, arrived, 0, [offset for offset in offsets if apart(offset) == 3])
    send(0, outgoing, arrived, 0, [offset for offset in offsets if apart(offset) <= 1])
    send(1, outgoing, arrived, 1)

    load_l.wait()
    load_r.wait()

    def precondition(s):
        def widen(i, carry):
            wide[pl.ds(pl.multiple_of(i * 128, 128), 128), :] = (
                arrived[s, pl.ds(i * 8, 8)].astype(jnp.float32).reshape(128, LANES)
            )
            return carry

        lax.fori_loop(0, DEVICES // 8, widen, 0)
        squares = jnp.zeros((8, LANES), jnp.float32)
        for j in range(ORDER // LANES):
            part = wide[pl.ds(j, ORDER, stride=4), :]
            squares += jnp.sum((part * part).reshape(ORDER // 8, 8, LANES), axis=0)
            tiles[s, :, j * LANES : (j + 1) * LANES] = part.astype(jnp.bfloat16)
        half[...] = jnp.dot(roots_l[s], tiles[s], preferred_element_type=jnp.float32).astype(jnp.bfloat16)
        shaped_squares = jnp.zeros((8, LANES), jnp.float32)
        for n in range(2):
            shaped = jnp.dot(
                half[...], roots_r[s, :, n * 256 : (n + 1) * 256], preferred_element_type=jnp.float32
            )
            for m in range(2):
                part = shaped[:, m * LANES : (m + 1) * LANES]
                shaped_squares += jnp.sum((part * part).reshape(ORDER // 8, 8, LANES), axis=0)
                wide[pl.ds(n * 2 + m, ORDER, stride=4), :] = part
        grad_norm = jnp.sqrt(jnp.sum(squares, keepdims=True))
        shaped_norm = jnp.sqrt(jnp.sum(shaped_squares, keepdims=True))
        scale = grad_norm / (shaped_norm + epsilon)

        def pack(i, carry):
            moved[s, pl.ds(i * 8, 8)] = (
                (wide[pl.ds(pl.multiple_of(i * 128, 128), 128), :] * scale)
                .astype(jnp.bfloat16)
                .reshape(8, ROWS, LANES)
            )
            return carry

        lax.fori_loop(0, DEVICES // 8, pack, 0)

    for s in range(SLOTS):
        wait(recv_sem, s, arrived, s)
        precondition(s)
        send(2 + s, moved, returned, s)
        returned[s, me] = moved[s, me]

    load_sl.wait()
    load_sr.wait()
    for s in range(SLOTS):
        tile = tiles[s]
        new_left[s] = decay_rate * left_in[s] + lax.dot_general(
            tile, tile, (((1,), (1,)), ((), ())), preferred_element_type=jnp.float32
        )
        new_right[s] = decay_rate * right_in[s] + lax.dot_general(
            tile, tile, (((0,), (0,)), ((), ())), preferred_element_type=jnp.float32
        )
    wait(recv_sem, 2, returned, 0)
    wait(recv_sem, 3, returned, 1)
    for s in range(SLOTS):
        wait(send_sem, s, outgoing, s)
        wait(send_sem, 2 + s, moved, s)


def finish(blocks_in, returned, left, right, direction, new_left, new_right, wide_out, rows_out, slot_block, out_sem):
    copies = [
        pltpu.make_async_copy(source.at[s], target.at[s], out_sem.at[2 * i + s])
        for i, (source, target) in enumerate(((left, new_left), (right, new_right)))
        for s in range(SLOTS)
    ]
    for copy in copies:
        copy.start()

    fetch = pltpu.make_async_copy(blocks_in, slot_block, out_sem.at[5])
    fetch.start()
    fetch.wait()

    def place(d, carry):
        for s in range(SLOTS):
            block = slot_block[d * SLOTS + s]
            wide_out[jnp.where(block < 0, BLOCKS, block)] = returned[s, d].astype(jnp.float32)
        return carry

    lax.fori_loop(0, DEVICES, place, 0, unroll=8)
    rows = wide_out.reshape((BLOCKS + 1) * ROWS, LANES)
    for j in range(ROWS):
        rows_out[:, j * LANES : (j + 1) * LANES] = rows[pl.ds(j, BLOCKS, stride=ROWS), :].astype(jnp.bfloat16)
    last = pltpu.make_async_copy(rows_out, direction, out_sem.at[4])
    last.start()
    for copy in copies:
        copy.wait()
    last.wait()


def body(gradient, slot_block, left_statistics, right_statistics, root_left, root_right):
    anywhere = pl.BlockSpec(memory_space=pltpu.HBM)
    chunk = (ROWS, LANES)
    square = (SLOTS, ORDER, ORDER)
    flops = 2 * 4 * SLOTS * ORDER**3
    returned, left, right = pl.pallas_call(
        kernel,
        out_shape=(
            pltpu.VMEM((SLOTS, DEVICES) + chunk, jnp.bfloat16),
            pltpu.VMEM(square, jnp.float32),
            pltpu.VMEM(square, jnp.float32),
        ),
        in_specs=[anywhere] * 6,
        out_specs=tuple(pl.BlockSpec(memory_space=pltpu.VMEM) for _ in range(3)),
        scratch_shapes=[
            pltpu.VMEM((BLOCKS, ROWS * LANES), jnp.float32),
            pltpu.VMEM((BLOCKS * ROWS, LANES), jnp.float32),
            pltpu.VMEM((BLOCKS + 1,) + chunk, jnp.bfloat16),
            pltpu.VMEM((SLOTS, DEVICES) + chunk, jnp.bfloat16),
            pltpu.VMEM((SLOTS, DEVICES) + chunk, jnp.bfloat16),
            pltpu.VMEM((DEVICES * ROWS, LANES), jnp.float32),
            pltpu.VMEM(square, jnp.bfloat16),
            pltpu.VMEM((ORDER, ORDER), jnp.bfloat16),
            pltpu.VMEM((SLOTS, DEVICES) + chunk, jnp.bfloat16),
            pltpu.VMEM(square, jnp.float32),
            pltpu.VMEM(square, jnp.float32),
            pltpu.VMEM(square, jnp.bfloat16),
            pltpu.VMEM(square, jnp.bfloat16),
            pltpu.SMEM((DEVICES * SLOTS,), jnp.int32),
            pltpu.SemaphoreType.DMA((4,)),
            pltpu.SemaphoreType.DMA((2,)),
            pltpu.SemaphoreType.DMA((4,)),
            pltpu.SemaphoreType.DMA((4,)),
            pltpu.SemaphoreType.REGULAR,
        ],
        compiler_params=pltpu.CompilerParams(
            collective_id=0, has_side_effects=True, vmem_limit_bytes=56 * 2**20
        ),
        cost_estimate=pl.CostEstimate(flops=flops, bytes_accessed=12 * 2**20, transcendentals=0),
    )(slot_block, gradient, left_statistics, right_statistics, root_left, root_right)
    in_vmem = pl.BlockSpec(memory_space=pltpu.VMEM)
    return pl.pallas_call(
        finish,
        out_shape=(
            jax.ShapeDtypeStruct((BLOCKS, ROWS * LANES), jnp.bfloat16),
            jax.ShapeDtypeStruct(square, jnp.float32),
            jax.ShapeDtypeStruct(square, jnp.float32),
        ),
        in_specs=[anywhere] + [in_vmem] * 3,
        out_specs=(anywhere,) * 3,
        scratch_shapes=[
            pltpu.VMEM((BLOCKS + 1,) + chunk, jnp.float32),
            pltpu.VMEM((BLOCKS, ROWS * LANES), jnp.bfloat16),
            pltpu.SMEM((DEVICES * SLOTS,), jnp.int32),
            pltpu.SemaphoreType.DMA((6,)),
        ],
        compiler_params=pltpu.CompilerParams(vmem_limit_bytes=16 * 2**20),
    )(slot_block, returned, left, right)


def solution(mesh):
    placed = (
        P(None, ("grp", "fsdp")),
        P(),
        P(("grp", "fsdp"), None, None),
        P(("grp", "fsdp"), None, None),
        P(("grp", "fsdp"), None, None),
        P(("grp", "fsdp"), None, None),
    )
    return jax.shard_map(
        body,
        mesh=mesh,
        in_specs=placed,
        out_specs=(
            P(None, ("grp", "fsdp")),
            P(("grp", "fsdp"), None, None),
            P(("grp", "fsdp"), None, None),
        ),
        check_vma=False,
    )
```

```python
import jax
import jax.numpy as jnp
from jax import lax
from jax.experimental import pallas as pl
from jax.experimental.pallas import tpu as pltpu
from jax.sharding import PartitionSpec as P

decay_rate = 0.95
epsilon = 1e-06

BLOCKS = 128
SLOTS = 2
ORDER = 512
ROWS, LANES = 16, 128
GROUPS, Y, X, CORES = 4, 4, 4, 2
DEVICES = GROUPS * Y * X * CORES
LOGICAL = pl.DeviceIdType.LOGICAL


def far_first():
    ring = (0, 1, 2, 1)

    def hops(offset):
        return ring[offset // 32] + ring[offset // 8 % 4] + ring[offset // 2 % 4] + 0.1 * (offset % 2)

    return sorted(range(1, DEVICES), key=lambda offset: (-hops(offset), offset))


def apart(offset):
    return sum(step > 0 for step in (offset // 32, offset // 8 % 4, offset // 2 % 4))


def kernel(
    blocks_in, gradient, left_stat, right_stat, root_left, root_right,
    returned, new_left, new_right,
    rows_in, chunks_wide, chunks, outgoing, arrived, wide, tiles, half, moved,
    left_in, right_in, roots_l, roots_r, slot_block,
    load_sem, stat_sem, send_sem, recv_sem, round_sem,
):
    g = lax.axis_index("grp")
    f = lax.axis_index("fsdp")
    me = g * 32 + f
    y, x, c = f // 8, lax.rem(f // 2, 4), lax.rem(f, 2)
    zs = [lax.rem(g + i, 4) * 32 for i in range(4)]
    ys = [lax.rem(y + i, 4) * 8 for i in range(4)]
    xs = [lax.rem(x + i, 4) * 2 for i in range(4)]
    cs = [lax.rem(c + i, 2) for i in range(2)]
    zy = [[a + b for b in ys] for a in zs]
    xc = [[a + b for b in cs] for a in xs]
    offsets = far_first()

    def device(offset):
        return zy[offset // 32][offset // 8 % 4] + xc[offset // 2 % 4][offset % 2]

    load = pltpu.make_async_copy(gradient, rows_in, load_sem.at[0])
    load.start()
    fetch = pltpu.make_async_copy(blocks_in, slot_block, load_sem.at[3])
    fetch.start()
    barrier = pltpu.get_barrier_semaphore()
    near = [offset for offset in offsets if apart(offset) <= 2]
    lines = [2, 4, 6]
    for offset in near:
        pl.semaphore_signal(barrier, inc=1, device_id=device(offset), device_id_type=LOGICAL)
    load_l = pltpu.make_async_copy(root_left, roots_l, load_sem.at[1])
    load_r = pltpu.make_async_copy(root_right, roots_r, load_sem.at[2])
    load_sl = pltpu.make_async_copy(left_stat, left_in, stat_sem.at[0])
    load_sr = pltpu.make_async_copy(right_stat, right_in, stat_sem.at[1])
    load_l.start()
    load_r.start()
    load_sl.start()
    load_sr.start()

    chunks[BLOCKS] = jnp.zeros((ROWS, LANES), jnp.bfloat16)
    load.wait()
    for j in range(ROWS):
        chunks_wide[pl.ds(j, BLOCKS, stride=ROWS), :] = rows_in[:, j * LANES : (j + 1) * LANES]

    def narrow(i, carry):
        chunks[pl.ds(i * 8, 8)] = (
            chunks_wide[pl.ds(pl.multiple_of(i * 128, 128), 128), :].astype(jnp.bfloat16).reshape(8, ROWS, LANES)
        )
        return carry

    lax.fori_loop(0, BLOCKS // 8, narrow, 0)

    def stage(s):
        def one(d, carry):
            block = slot_block[d * SLOTS + s]
            outgoing[s, d] = chunks[jnp.where(block < 0, BLOCKS, block)]
            return carry

        lax.fori_loop(0, DEVICES, one, 0, unroll=8)

    def send(i, source, target, s, offsets=offsets):
        for offset in offsets:
            d = device(offset)
            pltpu.make_async_remote_copy(
                src_ref=source.at[s, d],
                dst_ref=target.at[s, me],
                send_sem=send_sem.at[i],
                recv_sem=recv_sem.at[i],
                device_id=d,
                device_id_type=LOGICAL,
            ).start()

    def wait(sems, i, buffer, s):
        part = buffer.at[s, pl.ds(0, DEVICES - 1)]
        pltpu.make_async_copy(part, part, sems.at[i]).wait()

    fetch.wait()
    stage(0)
    stage(1)
    for s in range(SLOTS):
        arrived[s, me] = outgoing[s, me]
    pl.semaphore_wait(barrier, len(near))
    for offset in lines:
        pl.semaphore_signal(round_sem, inc=1, device_id=device(offset), device_id_type=LOGICAL)
    send(0, outgoing, arrived, 0, [offset for offset in offsets if apart(offset) == 2])
    pl.semaphore_wait(round_sem, len(lines))
    send(0, outgoing, arrived, 0, [offset for offset in offsets if apart(offset) == 3])
    send(0, outgoing, arrived, 0, [offset for offset in offsets if apart(offset) <= 1])
    send(1, outgoing, arrived, 1)

    load_l.wait()
    load_r.wait()

    def precondition(s):
        def widen(i, carry):
            wide[pl.ds(pl.multiple_of(i * 128, 128), 128), :] = (
                arrived[s, pl.ds(i * 8, 8)].astype(jnp.float32).reshape(128, LANES)
            )
            return carry

        lax.fori_loop(0, DEVICES // 8, widen, 0)
        squares = jnp.zeros((8, LANES), jnp.float32)
        for j in range(ORDER // LANES):
            part = wide[pl.ds(j, ORDER, stride=4), :]
            squares += jnp.sum((part * part).reshape(ORDER // 8, 8, LANES), axis=0)
            tiles[s, :, j * LANES : (j + 1) * LANES] = part.astype(jnp.bfloat16)
        half[...] = jnp.dot(roots_l[s], tiles[s], preferred_element_type=jnp.float32).astype(jnp.bfloat16)
        shaped_squares = jnp.zeros((8, LANES), jnp.float32)
        for n in range(2):
            shaped = jnp.dot(
                half[...], roots_r[s, :, n * 256 : (n + 1) * 256], preferred_element_type=jnp.float32
            )
            for m in range(2):
                part = shaped[:, m * LANES : (m + 1) * LANES]
                shaped_squares += jnp.sum((part * part).reshape(ORDER // 8, 8, LANES), axis=0)
                wide[pl.ds(n * 2 + m, ORDER, stride=4), :] = part
        grad_norm = jnp.sqrt(jnp.sum(squares, keepdims=True))
        shaped_norm = jnp.sqrt(jnp.sum(shaped_squares, keepdims=True))
        scale = grad_norm / (shaped_norm + epsilon)

        def pack(i, carry):
            moved[s, pl.ds(i * 8, 8)] = (
                (wide[pl.ds(pl.multiple_of(i * 128, 128), 128), :] * scale)
                .astype(jnp.bfloat16)
                .reshape(8, ROWS, LANES)
            )
            return carry

        lax.fori_loop(0, DEVICES // 8, pack, 0)

    for s in range(SLOTS):
        wait(recv_sem, s, arrived, s)
        precondition(s)
        send(2 + s, moved, returned, s)
        returned[s, me] = moved[s, me]

    load_sl.wait()
    load_sr.wait()
    for s in range(SLOTS):
        tile = tiles[s]
        new_left[s] = decay_rate * left_in[s] + lax.dot_general(
            tile, tile, (((1,), (1,)), ((), ())), preferred_element_type=jnp.float32
        )
        new_right[s] = decay_rate * right_in[s] + lax.dot_general(
            tile, tile, (((0,), (0,)), ((), ())), preferred_element_type=jnp.float32
        )
    wait(recv_sem, 2, returned, 0)
    wait(recv_sem, 3, returned, 1)
    for s in range(SLOTS):
        wait(send_sem, s, outgoing, s)
        wait(send_sem, 2 + s, moved, s)


def finish(blocks_in, returned, left, right, direction, new_left, new_right, wide_out, rows_out, slot_block, out_sem):
    copies = [
        pltpu.make_async_copy(source.at[s], target.at[s], out_sem.at[2 * i + s])
        for i, (source, target) in enumerate(((left, new_left), (right, new_right)))
        for s in range(SLOTS)
    ]
    for copy in copies:
        copy.start()

    fetch = pltpu.make_async_copy(blocks_in, slot_block, out_sem.at[5])
    fetch.start()
    fetch.wait()

    def place(d, carry):
        for s in range(SLOTS):
            block = slot_block[d * SLOTS + s]
            wide_out[jnp.where(block < 0, BLOCKS, block)] = returned[s, d].astype(jnp.float32)
        return carry

    lax.fori_loop(0, DEVICES, place, 0, unroll=8)
    rows = wide_out.reshape((BLOCKS + 1) * ROWS, LANES)
    for j in range(ROWS):
        rows_out[:, j * LANES : (j + 1) * LANES] = rows[pl.ds(j, BLOCKS, stride=ROWS), :].astype(jnp.bfloat16)
    last = pltpu.make_async_copy(rows_out, direction, out_sem.at[4])
    last.start()
    for copy in copies:
        copy.wait()
    last.wait()


def body(gradient, slot_block, left_statistics, right_statistics, root_left, root_right):
    anywhere = pl.BlockSpec(memory_space=pltpu.HBM)
    chunk = (ROWS, LANES)
    square = (SLOTS, ORDER, ORDER)
    flops = 2 * 4 * SLOTS * ORDER**3
    returned, left, right = pl.pallas_call(
        kernel,
        out_shape=(
            pltpu.VMEM((SLOTS, DEVICES) + chunk, jnp.bfloat16),
            pltpu.VMEM(square, jnp.float32),
            pltpu.VMEM(square, jnp.float32),
        ),
        in_specs=[anywhere] * 6,
        out_specs=tuple(pl.BlockSpec(memory_space=pltpu.VMEM) for _ in range(3)),
        scratch_shapes=[
            pltpu.VMEM((BLOCKS, ROWS * LANES), jnp.float32),
            pltpu.VMEM(((BLOCKS + 1) * ROWS, LANES), jnp.float32),
            pltpu.VMEM((BLOCKS + 1,) + chunk, jnp.bfloat16),
            pltpu.VMEM((SLOTS, DEVICES) + chunk, jnp.bfloat16),
            pltpu.VMEM((SLOTS, DEVICES) + chunk, jnp.bfloat16),
            pltpu.VMEM(((DEVICES + 1) * ROWS, LANES), jnp.float32),
            pltpu.VMEM(square, jnp.bfloat16),
            pltpu.VMEM((ORDER, ORDER), jnp.bfloat16),
            pltpu.VMEM((SLOTS, DEVICES) + chunk, jnp.bfloat16),
            pltpu.VMEM(square, jnp.float32),
            pltpu.VMEM(square, jnp.float32),
            pltpu.VMEM(square, jnp.bfloat16),
            pltpu.VMEM(square, jnp.bfloat16),
            pltpu.SMEM((DEVICES * SLOTS,), jnp.int32),
            pltpu.SemaphoreType.DMA((4,)),
            pltpu.SemaphoreType.DMA((2,)),
            pltpu.SemaphoreType.DMA((4,)),
            pltpu.SemaphoreType.DMA((4,)),
            pltpu.SemaphoreType.REGULAR,
        ],
        compiler_params=pltpu.CompilerParams(
            collective_id=0, has_side_effects=True, vmem_limit_bytes=56 * 2**20
        ),
        cost_estimate=pl.CostEstimate(flops=flops, bytes_accessed=12 * 2**20, transcendentals=0),
    )(slot_block, gradient, left_statistics, right_statistics, root_left, root_right)
    in_vmem = pl.BlockSpec(memory_space=pltpu.VMEM)
    return pl.pallas_call(
        finish,
        out_shape=(
            jax.ShapeDtypeStruct((BLOCKS, ROWS * LANES), jnp.bfloat16),
            jax.ShapeDtypeStruct(square, jnp.float32),
            jax.ShapeDtypeStruct(square, jnp.float32),
        ),
        in_specs=[anywhere] + [in_vmem] * 3,
        out_specs=(anywhere,) * 3,
        scratch_shapes=[
            pltpu.VMEM((BLOCKS + 1,) + chunk, jnp.float32),
            pltpu.VMEM((BLOCKS, ROWS * LANES), jnp.bfloat16),
            pltpu.SMEM((DEVICES * SLOTS,), jnp.int32),
            pltpu.SemaphoreType.DMA((6,)),
        ],
        compiler_params=pltpu.CompilerParams(vmem_limit_bytes=16 * 2**20),
    )(slot_block, returned, left, right)


def solution(mesh):
    placed = (
        P(None, ("grp", "fsdp")),
        P(),
        P(("grp", "fsdp"), None, None),
        P(("grp", "fsdp"), None, None),
        P(("grp", "fsdp"), None, None),
        P(("grp", "fsdp"), None, None),
    )
    return jax.shard_map(
        body,
        mesh=mesh,
        in_specs=placed,
        out_specs=(
            P(None, ("grp", "fsdp")),
            P(("grp", "fsdp"), None, None),
            P(("grp", "fsdp"), None, None),
        ),
        check_vma=False,
    )
```

```python
import jax
import jax.numpy as jnp
from jax import lax
from jax.experimental import pallas as pl
from jax.experimental.pallas import tpu as pltpu
from jax.sharding import PartitionSpec as P

decay_rate = 0.95
epsilon = 1e-06

BLOCKS = 128
SLOTS = 2
ORDER = 512
ROWS, LANES = 16, 128
GROUPS, Y, X, CORES = 4, 4, 4, 2
DEVICES = GROUPS * Y * X * CORES
LOGICAL = pl.DeviceIdType.LOGICAL


def far_first():
    ring = (0, 1, 2, 1)

    def hops(offset):
        return ring[offset // 32] + ring[offset // 8 % 4] + ring[offset // 2 % 4] + 0.1 * (offset % 2)

    return sorted(range(1, DEVICES), key=lambda offset: (-hops(offset), offset))


def apart(offset):
    return sum(step > 0 for step in (offset // 32, offset // 8 % 4, offset // 2 % 4))


def kernel(
    blocks_in, gradient, left_stat, right_stat, root_left, root_right,
    returned, new_left, new_right,
    rows_in, chunks_wide, chunks, outgoing, arrived, wide, tiles, half, moved,
    left_in, right_in, roots_l, roots_r, slot_block,
    load_sem, stat_sem, send_sem, recv_sem, round_sem,
):
    g = lax.axis_index("grp")
    f = lax.axis_index("fsdp")
    me = g * 32 + f
    y, x, c = f // 8, lax.rem(f // 2, 4), lax.rem(f, 2)
    zs = [lax.rem(g + i, 4) * 32 for i in range(4)]
    ys = [lax.rem(y + i, 4) * 8 for i in range(4)]
    xs = [lax.rem(x + i, 4) * 2 for i in range(4)]
    cs = [lax.rem(c + i, 2) for i in range(2)]
    zy = [[a + b for b in ys] for a in zs]
    xc = [[a + b for b in cs] for a in xs]
    offsets = far_first()

    def device(offset):
        return zy[offset // 32][offset // 8 % 4] + xc[offset // 2 % 4][offset % 2]

    barrier = pltpu.get_barrier_semaphore()
    near = [offset for offset in offsets if apart(offset) <= 2]
    lines = [2, 4, 6]
    for offset in near:
        pl.semaphore_signal(barrier, inc=1, device_id=device(offset), device_id_type=LOGICAL)
    load = pltpu.make_async_copy(gradient, rows_in, load_sem.at[0])
    load.start()
    fetch = pltpu.make_async_copy(blocks_in, slot_block, load_sem.at[3])
    fetch.start()
    load_l = pltpu.make_async_copy(root_left, roots_l, load_sem.at[1])
    load_r = pltpu.make_async_copy(root_right, roots_r, load_sem.at[2])
    load_sl = pltpu.make_async_copy(left_stat, left_in, stat_sem.at[0])
    load_sr = pltpu.make_async_copy(right_stat, right_in, stat_sem.at[1])
    load_l.start()
    load_r.start()
    load_sl.start()
    load_sr.start()

    chunks[BLOCKS] = jnp.zeros((ROWS, LANES), jnp.bfloat16)
    load.wait()
    for j in range(ROWS):
        chunks_wide[pl.ds(j, BLOCKS, stride=ROWS), :] = rows_in[:, j * LANES : (j + 1) * LANES]

    def narrow(i, carry):
        chunks[pl.ds(i * 8, 8)] = (
            chunks_wide[pl.ds(pl.multiple_of(i * 128, 128), 128), :].astype(jnp.bfloat16).reshape(8, ROWS, LANES)
        )
        return carry

    lax.fori_loop(0, BLOCKS // 8, narrow, 0)

    def stage(s):
        def one(d, carry):
            block = slot_block[d * SLOTS + s]
            outgoing[s, d] = chunks[jnp.where(block < 0, BLOCKS, block)]
            return carry

        lax.fori_loop(0, DEVICES, one, 0, unroll=8)

    def send(i, source, target, s, offsets=offsets):
        for offset in offsets:
            d = device(offset)
            pltpu.make_async_remote_copy(
                src_ref=source.at[s, d],
                dst_ref=target.at[s, me],
                send_sem=send_sem.at[i],
                recv_sem=recv_sem.at[i],
                device_id=d,
                device_id_type=LOGICAL,
            ).start()

    def wait(sems, i, buffer, s):
        part = buffer.at[s, pl.ds(0, DEVICES - 1)]
        pltpu.make_async_copy(part, part, sems.at[i]).wait()

    fetch.wait()
    stage(0)
    stage(1)
    for s in range(SLOTS):
        arrived[s, me] = outgoing[s, me]
    pl.semaphore_wait(barrier, len(near))
    for offset in lines:
        pl.semaphore_signal(round_sem, inc=1, device_id=device(offset), device_id_type=LOGICAL)
    send(0, outgoing, arrived, 0, [offset for offset in offsets if apart(offset) == 2])
    pl.semaphore_wait(round_sem, len(lines))
    send(0, outgoing, arrived, 0, [offset for offset in offsets if apart(offset) == 3])
    send(0, outgoing, arrived, 0, [offset for offset in offsets if apart(offset) <= 1])
    send(1, outgoing, arrived, 1)

    load_l.wait()
    load_r.wait()

    def precondition(s):
        def widen(i, carry):
            wide[pl.ds(pl.multiple_of(i * 128, 128), 128), :] = (
                arrived[s, pl.ds(i * 8, 8)].astype(jnp.float32).reshape(128, LANES)
            )
            return carry

        lax.fori_loop(0, DEVICES // 8, widen, 0)
        squares = jnp.zeros((8, LANES), jnp.float32)
        for j in range(ORDER // LANES):
            part = wide[pl.ds(j, ORDER, stride=4), :]
            squares += jnp.sum((part * part).reshape(ORDER // 8, 8, LANES), axis=0)
            tiles[s, :, j * LANES : (j + 1) * LANES] = part.astype(jnp.bfloat16)
        half[...] = jnp.dot(roots_l[s], tiles[s], preferred_element_type=jnp.float32).astype(jnp.bfloat16)
        shaped_squares = jnp.zeros((8, LANES), jnp.float32)
        for n in range(2):
            shaped = jnp.dot(
                half[...], roots_r[s, :, n * 256 : (n + 1) * 256], preferred_element_type=jnp.float32
            )
            for m in range(2):
                part = shaped[:, m * LANES : (m + 1) * LANES]
                shaped_squares += jnp.sum((part * part).reshape(ORDER // 8, 8, LANES), axis=0)
                wide[pl.ds(n * 2 + m, ORDER, stride=4), :] = part
        grad_norm = jnp.sqrt(jnp.sum(squares, keepdims=True))
        shaped_norm = jnp.sqrt(jnp.sum(shaped_squares, keepdims=True))
        scale = grad_norm / (shaped_norm + epsilon)

        def pack(i, carry):
            moved[s, pl.ds(i * 8, 8)] = (
                (wide[pl.ds(pl.multiple_of(i * 128, 128), 128), :] * scale)
                .astype(jnp.bfloat16)
                .reshape(8, ROWS, LANES)
            )
            return carry

        lax.fori_loop(0, DEVICES // 8, pack, 0)

    for s in range(SLOTS):
        wait(recv_sem, s, arrived, s)
        precondition(s)
        send(2 + s, moved, returned, s)
        returned[s, me] = moved[s, me]

    load_sl.wait()
    load_sr.wait()
    for s in range(SLOTS):
        tile = tiles[s]
        new_left[s] = decay_rate * left_in[s] + lax.dot_general(
            tile, tile, (((1,), (1,)), ((), ())), preferred_element_type=jnp.float32
        )
        new_right[s] = decay_rate * right_in[s] + lax.dot_general(
            tile, tile, (((0,), (0,)), ((), ())), preferred_element_type=jnp.float32
        )
    wait(recv_sem, 2, returned, 0)
    wait(recv_sem, 3, returned, 1)
    for s in range(SLOTS):
        wait(send_sem, s, outgoing, s)
        wait(send_sem, 2 + s, moved, s)


def finish(blocks_in, returned, left, right, direction, new_left, new_right, wide_out, rows_out, slot_block, out_sem):
    copies = [
        pltpu.make_async_copy(source.at[s], target.at[s], out_sem.at[2 * i + s])
        for i, (source, target) in enumerate(((left, new_left), (right, new_right)))
        for s in range(SLOTS)
    ]
    for copy in copies:
        copy.start()

    fetch = pltpu.make_async_copy(blocks_in, slot_block, out_sem.at[5])
    fetch.start()
    fetch.wait()

    def place(d, carry):
        for s in range(SLOTS):
            block = slot_block[d * SLOTS + s]
            wide_out[jnp.where(block < 0, BLOCKS, block)] = returned[s, d].astype(jnp.float32)
        return carry

    lax.fori_loop(0, DEVICES, place, 0, unroll=8)
    rows = wide_out.reshape((BLOCKS + 1) * ROWS, LANES)
    for j in range(ROWS):
        rows_out[:, j * LANES : (j + 1) * LANES] = rows[pl.ds(j, BLOCKS, stride=ROWS), :].astype(jnp.bfloat16)
    last = pltpu.make_async_copy(rows_out, direction, out_sem.at[4])
    last.start()
    for copy in copies:
        copy.wait()
    last.wait()


def body(gradient, slot_block, left_statistics, right_statistics, root_left, root_right):
    anywhere = pl.BlockSpec(memory_space=pltpu.HBM)
    chunk = (ROWS, LANES)
    square = (SLOTS, ORDER, ORDER)
    flops = 2 * 4 * SLOTS * ORDER**3
    returned, left, right = pl.pallas_call(
        kernel,
        out_shape=(
            pltpu.VMEM((SLOTS, DEVICES) + chunk, jnp.bfloat16),
            pltpu.VMEM(square, jnp.float32),
            pltpu.VMEM(square, jnp.float32),
        ),
        in_specs=[anywhere] * 6,
        out_specs=tuple(pl.BlockSpec(memory_space=pltpu.VMEM) for _ in range(3)),
        scratch_shapes=[
            pltpu.VMEM((BLOCKS, ROWS * LANES), jnp.float32),
            pltpu.VMEM(((BLOCKS + 1) * ROWS, LANES), jnp.float32),
            pltpu.VMEM((BLOCKS + 1,) + chunk, jnp.bfloat16),
            pltpu.VMEM((SLOTS, DEVICES) + chunk, jnp.bfloat16),
            pltpu.VMEM((SLOTS, DEVICES) + chunk, jnp.bfloat16),
            pltpu.VMEM(((DEVICES + 1) * ROWS, LANES), jnp.float32),
            pltpu.VMEM(square, jnp.bfloat16),
            pltpu.VMEM((ORDER, ORDER), jnp.bfloat16),
            pltpu.VMEM((SLOTS, DEVICES) + chunk, jnp.bfloat16),
            pltpu.VMEM(square, jnp.float32),
            pltpu.VMEM(square, jnp.float32),
            pltpu.VMEM(square, jnp.bfloat16),
            pltpu.VMEM(square, jnp.bfloat16),
            pltpu.SMEM((DEVICES * SLOTS,), jnp.int32),
            pltpu.SemaphoreType.DMA((4,)),
            pltpu.SemaphoreType.DMA((2,)),
            pltpu.SemaphoreType.DMA((4,)),
            pltpu.SemaphoreType.DMA((4,)),
            pltpu.SemaphoreType.REGULAR,
        ],
        compiler_params=pltpu.CompilerParams(
            collective_id=0, has_side_effects=True, vmem_limit_bytes=56 * 2**20
        ),
        cost_estimate=pl.CostEstimate(flops=flops, bytes_accessed=12 * 2**20, transcendentals=0),
    )(slot_block, gradient, left_statistics, right_statistics, root_left, root_right)
    in_vmem = pl.BlockSpec(memory_space=pltpu.VMEM)
    return pl.pallas_call(
        finish,
        out_shape=(
            jax.ShapeDtypeStruct((BLOCKS, ROWS * LANES), jnp.bfloat16),
            jax.ShapeDtypeStruct(square, jnp.float32),
            jax.ShapeDtypeStruct(square, jnp.float32),
        ),
        in_specs=[anywhere] + [in_vmem] * 3,
        out_specs=(anywhere,) * 3,
        scratch_shapes=[
            pltpu.VMEM((BLOCKS + 1,) + chunk, jnp.float32),
            pltpu.VMEM((BLOCKS, ROWS * LANES), jnp.bfloat16),
            pltpu.SMEM((DEVICES * SLOTS,), jnp.int32),
            pltpu.SemaphoreType.DMA((6,)),
        ],
        compiler_params=pltpu.CompilerParams(vmem_limit_bytes=16 * 2**20),
    )(slot_block, returned, left, right)


def solution(mesh):
    placed = (
        P(None, ("grp", "fsdp")),
        P(),
        P(("grp", "fsdp"), None, None),
        P(("grp", "fsdp"), None, None),
        P(("grp", "fsdp"), None, None),
        P(("grp", "fsdp"), None, None),
    )
    return jax.shard_map(
        body,
        mesh=mesh,
        in_specs=placed,
        out_specs=(
            P(None, ("grp", "fsdp")),
            P(("grp", "fsdp"), None, None),
            P(("grp", "fsdp"), None, None),
        ),
        check_vma=False,
    )
```
